32 devices in a mesh: req: 8 (over y, x, core), kv: 4 (over z).
Axes of the slice: x: 2, y: 2, z: 4, core: 2. Of those that a mesh axis runs over, the one named last changes fastest.
Arguments:
- hidden_in: bfloat16 [512, 5120], P('req'), may hold values from -6 to 6
- norm_gain: bfloat16 [5120], replicated, may hold values from 0.25 to 1.75
- w_query: bfloat16 [5120, 5120], P(None, 'kv'), may hold values from -1 to 1
- key_projection: bfloat16 [5120, 1024], P(None, 'kv'), may hold values from -4 to 4
- value_projection: bfloat16 [5120, 1024], P(None, 'kv'), may hold values from -0.15625 to 0.15625
- w_out: bfloat16 [5120, 5120], P('kv'), may hold values from -0.3125 to 0.3125
- pre_keys: bfloat16 [48, 2048, 1024], P('req', None, 'kv'), may hold values from -360 to 360
- prompt_values: bfloat16 [48, 2048, 1024], P('req', None, 'kv'), may hold values from -18 to 18
- continuation_keys: bfloat16 [512, 64, 1024], P('req', None, 'kv'), may hold values from -12 to 12
- continuation_values: bfloat16 [512, 64, 1024], P('req', None, 'kv'), may hold values from -18 to 18
- group_seq: int32 [512], replicated, may hold values from 0 to 47, never falling along the last dimension, each value on 1 to 16 neighbouring positions
- request_order: int32 [512], replicated, may hold values from 0 to 511, each once
- pre_len: int32 [48], replicated, may hold values from 1 to 2048, 73728 in all
- continuation_length: int32 [512], P('req'), may hold values from 1 to 64, 16384 in all
Outputs:
- attn_out: bfloat16 [512, 5120], P('req', 'kv')
The draws below stay inside these ranges and needn't reach their ends.
Inputs may be any that keep to these rules, and one draw needn't show every extreme that they name: `group_seq`: group numbers never fall along the list; each group holds 1 to 16 requests, and some group exactly 16. `request_order`: each request once. `pre_len`: some group has exactly 2048. `continuation_length`: some request has exactly 64.
All inputs are finite; a program needn't handle non-finite values. No bound on the sum of `continuation_length` on one device may be relied on, other than what follows from the above.
Results may differ from the reference program's by a relative error of at most 0.012.
The reference program's roundings to bfloat16 on the way count: a program that leaves them out, or rounds other values in their place, can miss the bound.
Values may be sent and summed in bfloat16 or wider, within the bound.
A program may use at most 192 MiB of HBM per device.

```python
import math
import jax
import jax.numpy as jnp
import numpy as np
from jax import lax

MODEL_WIDTH = 5120
QUERY_HEADS = 40
KEY_VALUE_HEADS = 8
HEAD_SIZE = 128
QUERY_PER_KEY = 5
GROUP_CAPACITY = 16
PROMPT_POSITIONS = 2048
TAIL_POSITIONS = 64
REQUEST_TOTAL = 512
GROUP_TOTAL = 48


def weight_base(key):
    raw_key = jax.random.fold_in(key, 31)
    shape = (MODEL_WIDTH, QUERY_HEADS * HEAD_SIZE)
    base = jnp.clip(jax.random.normal(raw_key, shape, jnp.float32), -4.5, 4.5)
    return base * MODEL_WIDTH ** (-0.5)


def draw_w_query(key, part):
    return weight_base(key).astype(jnp.bfloat16)


def draw_key_projection(key, part):
    base = weight_base(key).reshape(MODEL_WIDTH, KEY_VALUE_HEADS, QUERY_PER_KEY, HEAD_SIZE)
    shared = jnp.mean(base, axis=2).reshape(MODEL_WIDTH, KEY_VALUE_HEADS * HEAD_SIZE)
    noise_key = jax.random.fold_in(key, 47)
    noise = jnp.clip(jax.random.normal(noise_key, (MODEL_WIDTH, KEY_VALUE_HEADS * HEAD_SIZE), jnp.float32), -4.5, 4.5) * MODEL_WIDTH ** (-0.5)
    return (3.5 * shared + noise).astype(jnp.bfloat16)


def draw_pre_keys(key, part):
    leading_index = jax.random.fold_in(jax.random.fold_in(key, 11), 0)
    start_offset = jnp.clip(2.0 * jax.random.normal(leading_index, (GROUP_TOTAL, PROMPT_POSITIONS, KEY_VALUE_HEADS * HEAD_SIZE), jnp.float32), -12.0, 12.0)
    return start_offset.astype(jnp.bfloat16)


def level_of(rng, dims, cuts, smallest, high):
    level, own = 1.0, jax.random.fold_in(rng, 6)
    for position, blocks in cuts:
        draws = jnp.exp(jax.random.uniform(jax.random.fold_in(own, position), (blocks,), jnp.float32, smallest / len(cuts), high / len(cuts)))
        level = level * jnp.repeat(draws, dims[position] // blocks).reshape([-1 if axis == position else 1 for axis in range(len(dims))])
    return level


def profile(count, total, most, skew):
    weights = [(1 << 20) // math.isqrt(standing ** skew) + 1 for standing in range(2, count + 1)]
    rest, holding = total - most - (count - 1), [1] * (count - 1)
    while rest > 0:
        free = [i for i in range(count - 1) if holding[i] < most]
        pool, remaining = sum([weights[i] for i in free]), rest
        for i in free:
            addition = min(most - holding[i], max(1, remaining * weights[i] // pool), rest)
            holding[i] = holding[i] + addition
            rest = rest - addition
    return np.array([most] + holding)


def ragged(key, amount, total, limit, lean):
    if amount == 2:
        one = jax.random.randint(key, (), max(1, total - limit), min(limit, total - 1) + 1)
        return jnp.stack([one, total - one])
    sizes = jnp.asarray(profile(amount, total, limit, lean), jnp.int32)
    pairs = (amount - 1) // 2
    source_of, sink = sizes[1:1 + 2 * pairs:2], sizes[2:2 + 2 * pairs:2]
    margin = jnp.minimum(source_of - 1, limit - sink)
    shifted = jax.random.randint(jax.random.fold_in(key, 1), (pairs,), 0, 1 << 20) % (margin + 1)
    sizes = sizes.at[1:1 + 2 * pairs:2].set(source_of - shifted).at[2:2 + 2 * pairs:2].set(sink + shifted)
    return sizes[jax.random.permutation(jax.random.fold_in(key, 2), amount)]


def normal_values(stream_key, dims, deviation, limit, pieces=(), kind=jnp.bfloat16):
    array = deviation * jax.random.normal(stream_key, dims, jnp.float32)
    if pieces:
        array = array * level_of(stream_key, dims, pieces, -0.22, 0.18)
    return jnp.clip(array, -limit, limit).astype(kind)


def setup_inputs(seed: int = 0) -> dict:
    key_list = jax.random.split(jax.random.key(seed), 15)
    return {
        "hidden_in": normal_values(key_list[0], (REQUEST_TOTAL, MODEL_WIDTH), 1.0, 6.0, ((0, 8),)),
        "norm_gain": jnp.clip(1.0 + 0.15 * jax.random.normal(key_list[1], (MODEL_WIDTH,), jnp.float32), 0.25, 1.75).astype(jnp.bfloat16),
        "w_query": draw_w_query(jax.random.fold_in(key_list[14], 71), 0),
        "key_projection": draw_key_projection(jax.random.fold_in(key_list[14], 71), 0),
        "value_projection": normal_values(key_list[4], (MODEL_WIDTH, KEY_VALUE_HEADS * HEAD_SIZE), (MODEL_WIDTH // 4) ** -0.5, 0.15625, ((1, 4),)),
        "w_out": normal_values(key_list[5], (QUERY_HEADS * HEAD_SIZE, MODEL_WIDTH), (QUERY_HEADS * HEAD_SIZE // 16) ** -0.5, 0.3125, ((0, 4),)),
        "pre_keys": draw_pre_keys(jax.random.fold_in(key_list[14], 71), 0),
        "prompt_values": normal_values(key_list[7], (GROUP_TOTAL, PROMPT_POSITIONS, KEY_VALUE_HEADS * HEAD_SIZE), 3.0, 18.0, ((0, 8), (2, 4))),
        "continuation_keys": normal_values(key_list[8], (REQUEST_TOTAL, TAIL_POSITIONS, KEY_VALUE_HEADS * HEAD_SIZE), 2.0, 12.0, ((0, 8), (2, 4))),
        "continuation_values": normal_values(key_list[9], (REQUEST_TOTAL, TAIL_POSITIONS, KEY_VALUE_HEADS * HEAD_SIZE), 3.0, 18.0, ((0, 8), (2, 4))),
        "group_seq": jnp.searchsorted(jnp.cumsum(ragged(key_list[10], GROUP_TOTAL, REQUEST_TOTAL, GROUP_CAPACITY, 1)), jnp.arange(REQUEST_TOTAL), side="right").astype(jnp.int32),
        "request_order": jax.random.permutation(key_list[11], REQUEST_TOTAL).astype(jnp.int32),
        "pre_len": ragged(key_list[12], GROUP_TOTAL, GROUP_TOTAL * PROMPT_POSITIONS * 3 // 4, PROMPT_POSITIONS, 1).astype(jnp.int32),
        "continuation_length": ragged(key_list[13], REQUEST_TOTAL, REQUEST_TOTAL * TAIL_POSITIONS // 2, TAIL_POSITIONS, 1).astype(jnp.int32),
    }


EPS = 1e-06
THETA = 1000000.0

def apply_rotary(value_rows, token_position):
    half = value_rows.shape[-1] // 2
    freq = jnp.exp(-math.log(THETA) * 2.0 * jnp.arange(half, dtype=jnp.float32) / value_rows.shape[-1])
    angle = token_position.astype(jnp.float32)[:, None] * freq[None, :]
    cosine = jnp.cos(angle)[:, None, :]
    sine = jnp.sin(angle)[:, None, :]
    leading_index = value_rows[..., :half]
    second = value_rows[..., half:]
    return jnp.concatenate([leading_index * cosine - second * sine, second * cosine + leading_index * sine], axis=-1)

def rounded(value_rows):
    return lax.optimization_barrier(value_rows.astype(jnp.bfloat16)).astype(jnp.float32)

def continuation_partial(query_vector, fresh_key, fresh_value, key_rows, value_rows, live_length):
    scale = 1.0 / math.sqrt(query_vector.shape[-1])
    query32 = query_vector.astype(jnp.float32)
    scores = jnp.einsum('rkgd,rtkd->rkgt', query32, key_rows.astype(jnp.float32)) * scale
    live = jnp.arange(key_rows.shape[1], dtype=jnp.int32)[None, None, None, :] < live_length[:, None, None, None]
    scores = jnp.where(live, scores, -jnp.inf)
    own = jnp.einsum('rkgd,rkd->rkg', query32, fresh_key.astype(jnp.float32)) * scale
    top = jnp.maximum(lax.optimization_barrier(jnp.max(scores, axis=-1)), own)
    weights = jnp.where(live, jnp.exp(scores - top[..., None]), 0.0)
    own_weight = jnp.exp(own - top)
    total = lax.optimization_barrier(jnp.sum(weights, axis=-1)) + own_weight
    numer = jnp.einsum('rkgt,rtkd->rkgd', rounded(weights), value_rows.astype(jnp.float32))
    numer = numer + rounded(own_weight)[..., None] * fresh_value.astype(jnp.float32)[:, :, None, :]
    return (numer / total[..., None], top + jnp.log(total))

def prompt_partial(query_vector, key_rows, value_rows, live_length):
    scale = 1.0 / math.sqrt(query_vector.shape[-1])
    scores = jnp.einsum('skgd,tkd->kgst', query_vector.astype(jnp.float32), key_rows.astype(jnp.float32)) * scale
    live = jnp.arange(key_rows.shape[0], dtype=jnp.int32)[None, None, None, :] < live_length
    scores = jnp.where(live, scores, -jnp.inf)
    top = lax.optimization_barrier(jnp.max(scores, axis=-1))
    weights = jnp.where(live, jnp.exp(scores - top[..., None]), 0.0)
    total = lax.optimization_barrier(jnp.sum(weights, axis=-1))
    numer = jnp.einsum('kgst,tkd->skgd', rounded(weights), value_rows.astype(jnp.float32))
    total_s = jnp.transpose(total, (2, 0, 1))
    attention_output = (numer / total_s[..., None]).astype(jnp.bfloat16)
    log_sum_exp = jnp.transpose(top, (2, 0, 1)) + jnp.log(total_s)
    return (attention_output, log_sum_exp)

def reference(hidden_in, norm_gain, w_query, key_projection, value_projection, w_out, pre_keys, prompt_values, continuation_keys, continuation_values, group_seq, request_order, pre_len, continuation_length):
    request_rows = hidden_in.shape[0]
    groups = pre_keys.shape[0]
    group_of = jnp.zeros((request_rows,), jnp.int32).at[request_order].set(group_seq)
    hidden32 = hidden_in.astype(jnp.float32)
    normalized_hidden = (hidden32 * lax.rsqrt(lax.optimization_barrier(jnp.mean(hidden32 * hidden32, axis=1, keepdims=True)) + EPS) * norm_gain.astype(jnp.float32)).astype(jnp.bfloat16)
    token_position = pre_len[group_of] + continuation_length
    query_vector = apply_rotary(jnp.dot(normalized_hidden, w_query, preferred_element_type=jnp.float32).reshape(request_rows, QUERY_HEADS, HEAD_SIZE), token_position).astype(jnp.bfloat16)
    fresh_key = apply_rotary(jnp.dot(normalized_hidden, key_projection, preferred_element_type=jnp.float32).reshape(request_rows, KEY_VALUE_HEADS, HEAD_SIZE), token_position).astype(jnp.bfloat16)
    fresh_value = jnp.dot(normalized_hidden, value_projection, preferred_element_type=jnp.float32).reshape(request_rows, KEY_VALUE_HEADS, HEAD_SIZE).astype(jnp.bfloat16)
    query_grouped4 = query_vector.reshape(request_rows, KEY_VALUE_HEADS, QUERY_PER_KEY, HEAD_SIZE)
    continuation_output, continuation_log_sum = continuation_partial(query_grouped4, fresh_key, fresh_value, continuation_keys.reshape(request_rows, TAIL_POSITIONS, KEY_VALUE_HEADS, HEAD_SIZE), continuation_values.reshape(request_rows, TAIL_POSITIONS, KEY_VALUE_HEADS, HEAD_SIZE), continuation_length)
    query_flattened = query_vector.reshape(request_rows, QUERY_HEADS * HEAD_SIZE).astype(jnp.float32)
    slot_ids = jnp.arange(GROUP_CAPACITY, dtype=jnp.int32)

    def visit(carry, item):
        gid, key_rows, value_rows, live_length = item
        member = group_of == gid
        rank = jnp.cumsum(member.astype(jnp.int32)) - 1
        select_group = (member[None, :] & (rank[None, :] == slot_ids[:, None])).astype(jnp.float32)
        selected_rows = jnp.dot(select_group, query_flattened, precision=lax.Precision.HIGHEST).astype(jnp.bfloat16).reshape(GROUP_CAPACITY, KEY_VALUE_HEADS, QUERY_PER_KEY, HEAD_SIZE)
        attention_output, log_sum_exp = prompt_partial(selected_rows, key_rows.reshape(PROMPT_POSITIONS, KEY_VALUE_HEADS, HEAD_SIZE), value_rows.reshape(PROMPT_POSITIONS, KEY_VALUE_HEADS, HEAD_SIZE), live_length)
        full_out = carry[0] + jnp.dot(select_group.T, attention_output.reshape(GROUP_CAPACITY, QUERY_HEADS * HEAD_SIZE).astype(jnp.float32), precision=lax.Precision.HIGHEST)
        full_lse = carry[1] + jnp.dot(select_group.T, log_sum_exp.reshape(GROUP_CAPACITY, QUERY_HEADS), precision=lax.Precision.HIGHEST)
        return ((full_out, full_lse), None)
    start = (jnp.zeros((request_rows, QUERY_HEADS * HEAD_SIZE), jnp.float32), jnp.zeros((request_rows, QUERY_HEADS), jnp.float32))
    (pre_out, pre_lse), _ = lax.scan(visit, start, (jnp.arange(groups, dtype=jnp.int32), pre_keys, prompt_values, pre_len))
    tail_lse2 = continuation_log_sum.reshape(request_rows, QUERY_HEADS)
    both = jnp.logaddexp(pre_lse, tail_lse2)
    attn = jnp.exp(pre_lse - both)[..., None] * pre_out.reshape(request_rows, QUERY_HEADS, HEAD_SIZE) + jnp.exp(tail_lse2 - both)[..., None] * continuation_output.reshape(request_rows, QUERY_HEADS, HEAD_SIZE)
    attn = attn.reshape(request_rows, QUERY_HEADS * HEAD_SIZE).astype(jnp.bfloat16)
    return jnp.dot(attn, w_out, preferred_element_type=jnp.float32).astype(jnp.bfloat16)
```

```python
import functools
import math

import jax
import jax.numpy as jnp
from jax import lax
from jax.experimental import pallas as pl
from jax.experimental.pallas import tpu as pltpu
from jax.sharding import PartitionSpec as P

HEAD_SIZE = 128
QUERY_PER_KEY = 5
GROUP_CAPACITY = 16
EPS = 1e-06
THETA = 1000000.0
NEG = -1e30
FAST_CAPACITY = 32
CHUNK_ROWS = 16

F32 = jnp.float32
BF16 = jnp.bfloat16
MESH = pl.DeviceIdType.MESH


def iota(shape, dim):
    return lax.broadcasted_iota(jnp.int32, shape, dim)


def to_row(col):
    n = col.shape[0]
    eye = iota((n, n), 0) == iota((n, n), 1)
    return jnp.sum(jnp.where(eye, col, 0.0), axis=0, keepdims=True)


def to_col(row):
    n = row.shape[1]
    eye = iota((n, n), 0) == iota((n, n), 1)
    return jnp.sum(jnp.where(eye, row, 0.0), axis=1, keepdims=True)


def onehot(mask):
    return jnp.where(mask, 1.0, 0.0).astype(BF16)


def body(
    cap,
    n,
    nkv,
    gain_ref,
    order_ref,
    group_ref,
    plen_ref,
    clen_ref,
    hidden_hbm,
    wq_hbm,
    wk_hbm,
    wv_hbm,
    wo_hbm,
    pk_hbm,
    pv_hbm,
    ck_hbm,
    cv_hbm,
    out_ref,
    hidden,
    normed,
    w,
    wo,
    pk,
    pv,
    ck,
    cv,
    qkv,
    sel,
    packed,
    sendq,
    recvq,
    sendo,
    recvo,
    tail_out,
    tail_lse,
    attn,
    zsend,
    zrecv,
    h_sem,
    w_sem,
    wo_sem,
    pk_sem,
    pv_sem,
    ck_sem,
    cv_sem,
    q_send_sem,
    q_recv_sem,
    o_send_sem,
    o_recv_sem,
    z_send_sem,
    z_recv_sem,
):
    rows = hidden.shape[0]
    lg = pk.shape[0]
    plen = pk.shape[1]
    chunk = w.shape[2]
    lkv = chunk // HEAD_SIZE
    heads = lkv * QUERY_PER_KEY
    qc = heads * HEAD_SIZE
    tcap = ck.shape[0] // rows
    oc = out_ref.shape[1]
    slots = lg * GROUP_CAPACITY
    total = order_ref.shape[1]
    scale = 1.0 / math.sqrt(HEAD_SIZE)
    me = lax.axis_index("req")
    mk = lax.axis_index("kv")

    h_copy = pltpu.make_async_copy(hidden_hbm, hidden, h_sem)
    h_copy.start()
    for i in range(QUERY_PER_KEY):
        pltpu.make_async_copy(wq_hbm.at[:, pl.ds(i * chunk, chunk)], w.at[i], w_sem.at[i]).start()
    pltpu.make_async_copy(wk_hbm, w.at[QUERY_PER_KEY], w_sem.at[QUERY_PER_KEY]).start()
    pltpu.make_async_copy(wv_hbm, w.at[QUERY_PER_KEY + 1], w_sem.at[QUERY_PER_KEY + 1]).start()

    barrier = pltpu.get_barrier_semaphore()
    for o in range(1, n):
        pl.semaphore_signal(
            barrier, inc=1, device_id=(lax.rem(me + o, n), mk), device_id_type=MESH
        )
    for o in range(1, nkv):
        pl.semaphore_signal(
            barrier, inc=1, device_id=(me, lax.rem(mk + o, nkv)), device_id_type=MESH
        )

    order = order_ref[...].astype(F32)
    groups = group_ref[...].astype(F32)
    plens = plen_ref[...].astype(F32)
    lane = iota((1, total), 1).astype(F32)

    own = iota((rows, 1), 0).astype(F32) + (me * rows).astype(F32)
    g_col = jnp.sum(jnp.where(order == own, groups, 0.0), axis=1, keepdims=True)
    all_g = iota((1, plens.shape[1]), 1).astype(F32)
    own_len = jnp.sum(jnp.where(all_g == g_col, plens, 0.0), axis=1, keepdims=True)
    position = own_len + clen_ref[...].astype(F32)
    d_col = jnp.floor((g_col + 0.5) * (1.0 / lg))
    d_row = to_row(d_col)
    earlier = (d_col == d_row) & (iota((rows, rows), 0) < iota((rows, rows), 1))
    t_row = d_row * cap + jnp.sum(jnp.where(earlier, 1.0, 0.0), axis=0, keepdims=True)
    t_col = to_col(t_row)
    to_send = onehot(iota((n * cap, rows), 0).astype(F32) == t_row)
    from_return = onehot(iota((rows, n * cap), 1).astype(F32) == t_col)

    slot = iota((slots, 1), 0).astype(F32)
    slot_g = jnp.floor((slot + 0.5) * (1.0 / GROUP_CAPACITY))
    slot_k = slot - slot_g * GROUP_CAPACITY
    slot_g = slot_g + (me * lg).astype(F32)
    start = jnp.sum(jnp.where(groups < slot_g, 1.0, 0.0), axis=1, keepdims=True)
    count = jnp.sum(jnp.where(groups == slot_g, 1.0, 0.0), axis=1, keepdims=True)
    r_col = jnp.sum(jnp.where(lane == start + slot_k, order, 0.0), axis=1, keepdims=True)
    live = slot_k < count
    s_col = jnp.where(live, jnp.floor((r_col + 0.5) * (1.0 / rows)), -1.0)
    same = (s_col == to_row(s_col)) & (to_row(r_col) < r_col)
    u_col = jnp.where(
        live, s_col * cap + jnp.sum(jnp.where(same, 1.0, 0.0), axis=1, keepdims=True), -1.0
    )
    from_query = onehot(iota((slots, n * cap), 1).astype(F32) == u_col)
    to_return = onehot(iota((n * cap, slots), 0).astype(F32) == to_row(u_col))

    half = HEAD_SIZE // 2
    lane_h = iota((1, HEAD_SIZE), 1)
    upper = lane_h >= half
    freq_index = jnp.where(upper, lane_h - half, lane_h).astype(F32)
    freq = jnp.exp(-math.log(THETA) * 2.0 * freq_index / HEAD_SIZE)
    angle = position * freq
    cosine = jnp.cos(angle)
    sine = jnp.where(upper, jnp.sin(angle), -jnp.sin(angle))

    h_copy.wait()
    h32 = hidden[...].astype(F32)
    inv = lax.rsqrt(jnp.mean(h32 * h32, axis=1, keepdims=True) + EPS)
    normed[...] = (h32 * inv * gain_ref[...].astype(F32)).astype(BF16)

    def project(i, carry):
        pltpu.make_async_copy(wk_hbm, w.at[i], w_sem.at[i]).wait()
        y = jnp.dot(normed[...], w[i], preferred_element_type=F32)
        for a in range(lkv):
            x = y[:, a * HEAD_SIZE : (a + 1) * HEAD_SIZE]
            turned = x * cosine + pltpu.roll(x, half, 1) * sine
            x = jnp.where(i == QUERY_PER_KEY + 1, x, turned)
            qkv[i, :, a * HEAD_SIZE : (a + 1) * HEAD_SIZE] = x.astype(BF16)
        return carry

    lax.fori_loop(0, 3, project, 0)
    pltpu.make_async_copy(ck_hbm, ck, ck_sem).start()
    pltpu.make_async_copy(cv_hbm, cv, cv_sem).start()
    for g in range(lg):
        pltpu.make_async_copy(pk_hbm.at[g], pk.at[g], pk_sem.at[g]).start()
        pltpu.make_async_copy(pv_hbm.at[g], pv.at[g], pv_sem.at[g]).start()
    for j in range(nkv):
        pltpu.make_async_copy(wo_hbm.at[:, pl.ds(j * oc, oc)], wo.at[j], wo_sem.at[j]).start()
    lax.fori_loop(3, QUERY_PER_KEY, project, 0)

    for i in range(QUERY_PER_KEY):
        sendq[:, i * chunk : (i + 1) * chunk] = jnp.dot(
            to_send, qkv[i], preferred_element_type=F32
        ).astype(BF16)
    pl.semaphore_wait(barrier, n - 1 + nkv - 1)

    def req_copy(src, dst, send_sem, recv_sem, o):
        to = lax.rem(me + o, n)
        return pltpu.make_async_remote_copy(
            src_ref=src.at[pl.ds(pl.multiple_of(to * cap, cap), cap)],
            dst_ref=dst.at[pl.ds(pl.multiple_of(me * cap, cap), cap)],
            send_sem=send_sem.at[o],
            recv_sem=recv_sem.at[me],
            device_id=(to, mk),
            device_id_type=MESH,
        )

    def req_arrival(src, dst, send_sem, recv_sem, o):
        frm = lax.rem(me + n - o, n)
        here = pl.ds(pl.multiple_of(frm * cap, cap), cap)
        return pltpu.make_async_remote_copy(
            src_ref=src.at[here],
            dst_ref=dst.at[here],
            send_sem=send_sem.at[o],
            recv_sem=recv_sem.at[frm],
            device_id=(frm, mk),
            device_id_type=MESH,
        )

    mine = pl.ds(pl.multiple_of(me * cap, cap), cap)
    for o in range(1, n):
        req_copy(sendq, recvq, q_send_sem, q_recv_sem, o).start()
    recvq[mine, :] = sendq[mine, :]

    lax.fori_loop(QUERY_PER_KEY, QUERY_PER_KEY + 2, project, 0)
    pltpu.make_async_copy(ck_hbm, ck, ck_sem).wait()
    pltpu.make_async_copy(cv_hbm, cv, cv_sem).wait()
    block = CHUNK_ROWS
    width = block * tcap
    q_rows = QUERY_PER_KEY * block
    lanes = iota((block, HEAD_SIZE), 1)
    row_r = lax.rem(iota((q_rows, 1), 0), block)
    low = row_r * tcap
    col_t = iota((1, width), 1)

    def own_part(b, carry):
        at = pl.ds(pl.multiple_of(b * block, block), block)
        kv_at = pl.ds(pl.multiple_of(b * width, width), width)
        length = clen_ref[at, :]
        length = jnp.concatenate([length] * QUERY_PER_KEY, axis=0)
        ok = (col_t >= low) & (col_t < low + length)
        lse_tile = jnp.zeros((block, HEAD_SIZE), F32)
        for k in range(lkv):
            ks = slice(k * HEAD_SIZE, (k + 1) * HEAD_SIZE)
            parts = []
            for h in range(QUERY_PER_KEY):
                head = k * QUERY_PER_KEY + h
                c, a = head // lkv, head % lkv
                parts.append(qkv[c, at, a * HEAD_SIZE : (a + 1) * HEAD_SIZE])
            q = jnp.concatenate(parts, axis=0)
            new_k = qkv[QUERY_PER_KEY, at, ks].astype(F32)
            new_v = qkv[QUERY_PER_KEY + 1, at, ks].astype(F32)
            s = lax.dot_general(
                q, ck[kv_at, ks], (((1,), (1,)), ((), ())), preferred_element_type=F32
            ) * scale
            s = jnp.where(ok, s, NEG)
            fresh = jnp.sum(
                q.astype(F32) * jnp.concatenate([new_k] * QUERY_PER_KEY, axis=0),
                axis=1,
                keepdims=True,
            ) * scale
            top = jnp.maximum(jnp.max(s, axis=1, keepdims=True), fresh)
            e = jnp.exp(s - top)
            fresh_e = jnp.exp(fresh - top)
            l = jnp.sum(e, axis=1, keepdims=True) + fresh_e
            acc = jnp.dot(e.astype(BF16), cv[kv_at, ks], preferred_element_type=F32)
            acc = acc + fresh_e.astype(BF16).astype(F32) * jnp.concatenate(
                [new_v] * QUERY_PER_KEY, axis=0
            )
            acc = acc / l
            lse = top + jnp.log(l)
            for h in range(QUERY_PER_KEY):
                head = k * QUERY_PER_KEY + h
                rs = slice(h * block, (h + 1) * block)
                tail_out[at, head * HEAD_SIZE : (head + 1) * HEAD_SIZE] = acc[rs]
                lse_tile = jnp.where(lanes == head, lse[rs], lse_tile)
        tail_lse[at, :] = lse_tile
        return carry

    lax.fori_loop(0, rows // block, own_part, 0)

    for o in range(1, n):
        req_arrival(sendq, recvq, q_send_sem, q_recv_sem, o).wait_recv()
    sel[...] = jnp.dot(from_query, recvq[...], preferred_element_type=F32).astype(BF16)

    cap_g = GROUP_CAPACITY
    lanes_g = iota((cap_g, HEAD_SIZE), 1)
    part_of = lanes_g // 32
    lane_of = lanes_g - part_of * 32
    col_p = iota((1, plen), 1).astype(F32)

    def prompt_part(g, carry):
        pltpu.make_async_copy(pk_hbm.at[g], pk.at[g], pk_sem.at[g]).wait()
        pltpu.make_async_copy(pv_hbm.at[g], pv.at[g], pv_sem.at[g]).wait()
        at = pl.ds(pl.multiple_of(g * cap_g, cap_g), cap_g)
        gid = (me * lg + g).astype(F32)
        length = jnp.sum(jnp.where(all_g == gid, plens, 0.0), axis=1, keepdims=True)
        ok = col_p < length
        lse_tile = jnp.zeros((cap_g, HEAD_SIZE), F32)
        for k in range(lkv):
            ks = slice(k * HEAD_SIZE, (k + 1) * HEAD_SIZE)
            q = jnp.concatenate(
                [
                    sel[at, (k * QUERY_PER_KEY + h) * HEAD_SIZE : (k * QUERY_PER_KEY + h + 1) * HEAD_SIZE]
                    for h in range(QUERY_PER_KEY)
                ],
                axis=0,
            )
            s = lax.dot_general(
                q, pk[g, :, ks], (((1,), (1,)), ((), ())), preferred_element_type=F32
            ) * scale
            s = jnp.where(ok, s, NEG)
            top = jnp.max(s, axis=1, keepdims=True)
            e = jnp.exp(s - top)
            l = jnp.sum(e, axis=1, keepdims=True)
            acc = jnp.dot(e.astype(BF16), pv[g, :, ks], preferred_element_type=F32) / l
            lse = top + jnp.log(l)
            for h in range(QUERY_PER_KEY):
                head = k * QUERY_PER_KEY + h
                rs = slice(h * cap_g, (h + 1) * cap_g)
                packed[at, head * HEAD_SIZE : (head + 1) * HEAD_SIZE] = acc[rs].astype(BF16)
                lse_tile = jnp.where(lane_of == head, lse[rs], lse_tile)
        hi = lse_tile.astype(BF16).astype(F32)
        mid = (lse_tile - hi).astype(BF16).astype(F32)
        low_part = lse_tile - hi - mid
        tile = jnp.where(part_of == 0, hi, jnp.where(part_of == 1, mid, low_part))
        packed[at, qc : qc + HEAD_SIZE] = jnp.where(part_of == 3, 0.0, tile).astype(BF16)
        return carry

    lax.fori_loop(0, lg, prompt_part, 0)

    sendo[...] = jnp.dot(to_return, packed[...], preferred_element_type=F32).astype(BF16)
    for o in range(1, n):
        req_copy(sendo, recvo, o_send_sem, o_recv_sem, o).start()
    recvo[mine, :] = sendo[mine, :]
    for j in range(nkv):
        pltpu.make_async_copy(
            wo_hbm.at[:, pl.ds(j * oc, oc)], wo.at[j], wo_sem.at[j]
        ).wait()
    for o in range(1, n):
        req_arrival(sendo, recvo, o_send_sem, o_recv_sem, o).wait_recv()
    got = jnp.dot(from_return, recvo[...], preferred_element_type=F32)

    parts = got[:, qc : qc + HEAD_SIZE]
    pre_lse = parts + pltpu.roll(parts, HEAD_SIZE - 32, 1) + pltpu.roll(parts, HEAD_SIZE - 64, 1)
    t_lse = tail_lse[...]
    top = jnp.maximum(pre_lse, t_lse)
    both = top + jnp.log(jnp.exp(pre_lse - top) + jnp.exp(t_lse - top))
    w_pre = jnp.exp(pre_lse - both)
    w_tail = jnp.exp(t_lse - both)
    for head in range(heads):
        hs = slice(head * HEAD_SIZE, (head + 1) * HEAD_SIZE)
        attn[:, hs] = (
            w_pre[:, head : head + 1] * got[:, hs] + w_tail[:, head : head + 1] * tail_out[:, hs]
        ).astype(BF16)

    def z_copy(o):
        return pltpu.make_async_remote_copy(
            src_ref=zsend.at[o - 1],
            dst_ref=zrecv.at[o - 1],
            send_sem=z_send_sem.at[o - 1],
            recv_sem=z_recv_sem.at[o - 1],
            device_id=(me, lax.rem(mk + o, nkv)),
            device_id_type=MESH,
        )

    for o in range(1, nkv):
        zsend[o - 1] = jnp.dot(
            attn[...], wo[lax.rem(mk + o, nkv)], preferred_element_type=F32
        ).astype(BF16)
        z_copy(o).start()
    acc = jnp.dot(attn[...], wo[mk], preferred_element_type=F32)
    for o in range(1, nkv):
        z_copy(o).wait_recv()
        acc = acc + zrecv[o - 1].astype(F32)
    out_ref[...] = acc.astype(BF16)
    for o in range(1, n):
        req_copy(sendq, recvq, q_send_sem, q_recv_sem, o).wait_send()
        req_copy(sendo, recvo, o_send_sem, o_recv_sem, o).wait_send()
    for o in range(1, nkv):
        z_copy(o).wait_send()


def attend(cap, n, nkv, cid, *arrays):
    (gain, order, group, plen, clen, hidden, wq, wk, wv, wo, pk, pv, ck, cv) = arrays
    rows, model = hidden.shape
    chunk = wk.shape[1]
    qc = wq.shape[1]
    oc = wo.shape[1] // nkv
    lg, positions = pk.shape[0], pk.shape[1]
    slots = lg * GROUP_CAPACITY
    wide = qc + HEAD_SIZE
    vmem = pl.BlockSpec(memory_space=pltpu.VMEM)
    hbm = pl.BlockSpec(memory_space=pl.ANY)
    dma = pltpu.SemaphoreType.DMA
    return pl.pallas_call(
        functools.partial(body, cap, n, nkv),
        out_shape=jax.ShapeDtypeStruct((rows, oc), BF16),
        in_specs=[vmem] * 5 + [hbm] * 9,
        out_specs=vmem,
        scratch_shapes=[
            pltpu.VMEM((rows, model), BF16),
            pltpu.VMEM((rows, model), BF16),
            pltpu.VMEM((QUERY_PER_KEY + 2, model, chunk), BF16),
            pltpu.VMEM((nkv, qc, oc), BF16),
            pltpu.VMEM(pk.shape, BF16),
            pltpu.VMEM(pv.shape, BF16),
            pltpu.VMEM(ck.shape, BF16),
            pltpu.VMEM(cv.shape, BF16),
            pltpu.VMEM((QUERY_PER_KEY + 2, rows, chunk), BF16),
            pltpu.VMEM((slots, qc), BF16),
            pltpu.VMEM((slots, wide), BF16),
            pltpu.VMEM((n * cap, qc), BF16),
            pltpu.VMEM((n * cap, qc), BF16),
            pltpu.VMEM((n * cap, wide), BF16),
            pltpu.VMEM((n * cap, wide), BF16),
            pltpu.VMEM((rows, qc), F32),
            pltpu.VMEM((rows, HEAD_SIZE), F32),
            pltpu.VMEM((rows, qc), BF16),
            pltpu.VMEM((nkv - 1, rows, oc), BF16),
            pltpu.VMEM((nkv - 1, rows, oc), BF16),
            dma,
            dma((QUERY_PER_KEY + 2,)),
            dma((nkv,)),
            dma((lg,)),
            dma((lg,)),
            dma,
            dma,
            dma((n,)),
            dma((n,)),
            dma((n,)),
            dma((n,)),
            dma((nkv - 1,)),
            dma((nkv - 1,)),
        ],
        compiler_params=pltpu.CompilerParams(
            collective_id=cid, has_side_effects=True, vmem_limit_bytes=62 * 1024 * 1024
        ),
        name="attend%d" % cap,
    )(*arrays)


def shards(
    hidden_in,
    norm_gain,
    w_query,
    key_projection,
    value_projection,
    w_out,
    pre_keys,
    prompt_values,
    continuation_keys,
    continuation_values,
    group_seq,
    request_order,
    pre_len,
    continuation_length,
):
    n = lax.axis_size("req")
    nkv = lax.axis_size("kv")
    rows = hidden_in.shape[0]
    lg = pre_keys.shape[0]
    width = continuation_keys.shape[2]
    arrays = (
        norm_gain[None, :],
        request_order[None, :],
        group_seq[None, :],
        pre_len[None, :],
        continuation_length[:, None],
        hidden_in,
        w_query,
        key_projection,
        value_projection,
        w_out,
        pre_keys,
        prompt_values,
        continuation_keys.reshape(-1, width),
        continuation_values.reshape(-1, width),
    )
    if rows <= FAST_CAPACITY:
        return attend(rows, n, nkv, 0, *arrays)
    pair = (request_order // rows) * n + group_seq // lg
    counts = jnp.sum(
        (pair[None, :] == jnp.arange(n * n, dtype=jnp.int32)[:, None]).astype(jnp.int32), axis=1
    )
    return lax.cond(
        jnp.max(counts) <= FAST_CAPACITY,
        functools.partial(attend, FAST_CAPACITY, n, nkv, 0),
        functools.partial(attend, rows, n, nkv, 1),
        *arrays,
    )


def solution(mesh):
    placed = (
        P("req", None),
        P(),
        P(None, "kv"),
        P(None, "kv"),
        P(None, "kv"),
        P("kv", None),
        P("req", None, "kv"),
        P("req", None, "kv"),
        P("req", None, "kv"),
        P("req", None, "kv"),
        P(),
        P(),
        P(),
        P("req"),
    )
    return jax.shard_map(
        shards, mesh=mesh, in_specs=placed, out_specs=P("req", "kv"), check_vma=False
    )
```

```python
import functools
import math

import jax
import jax.numpy as jnp
from jax import lax
from jax.experimental import pallas as pl
from jax.experimental.pallas import tpu as pltpu
from jax.sharding import PartitionSpec as P

HEAD_SIZE = 128
QUERY_PER_KEY = 5
GROUP_CAPACITY = 16
EPS = 1e-06
THETA = 1000000.0
NEG = -1e30
FAST_CAPACITY = 32
CHUNK_ROWS = 16

F32 = jnp.float32
BF16 = jnp.bfloat16
MESH = pl.DeviceIdType.MESH


def iota(shape, dim):
    return lax.broadcasted_iota(jnp.int32, shape, dim)


def to_row(col):
    n = col.shape[0]
    eye = iota((n, n), 0) == iota((n, n), 1)
    return jnp.sum(jnp.where(eye, col, 0.0), axis=0, keepdims=True)


def to_col(row):
    n = row.shape[1]
    eye = iota((n, n), 0) == iota((n, n), 1)
    return jnp.sum(jnp.where(eye, row, 0.0), axis=1, keepdims=True)


def onehot(mask):
    return jnp.where(mask, 1.0, 0.0).astype(BF16)


def body(
    cap,
    n,
    nkv,
    gain_ref,
    order_ref,
    group_ref,
    plen_ref,
    clen_ref,
    hidden_hbm,
    wq_hbm,
    wk_hbm,
    wv_hbm,
    wo_hbm,
    pk_hbm,
    pv_hbm,
    ck_hbm,
    cv_hbm,
    out_ref,
    hidden,
    normed,
    wq,
    wkv,
    wo,
    pk,
    pv,
    ck,
    cv,
    acc_q,
    query,
    new_kv,
    lengths,
    sel,
    packed,
    sendq,
    recvq,
    sendo,
    recvo,
    tail_out,
    tail_lse,
    attn,
    zsend,
    zrecv,
    h_sem,
    w_sem,
    wo_sem,
    pk_sem,
    pv_sem,
    ck_sem,
    cv_sem,
    q_send_sem,
    q_recv_sem,
    o_send_sem,
    o_recv_sem,
    z_send_sem,
    z_recv_sem,
):
    rows = hidden.shape[0]
    lg = pk.shape[0]
    plen = pk.shape[1]
    chunk = wkv.shape[2]
    lkv = chunk // HEAD_SIZE
    heads = lkv * QUERY_PER_KEY
    qc = heads * HEAD_SIZE
    tcap = ck.shape[0] // rows
    oc = out_ref.shape[1]
    slots = lg * GROUP_CAPACITY
    total = order_ref.shape[1]
    scale = 1.0 / math.sqrt(HEAD_SIZE)
    me = lax.axis_index("req")
    mk = lax.axis_index("kv")

    h_copy = pltpu.make_async_copy(hidden_hbm, hidden, h_sem)
    h_copy.start()
    k_rows = hidden.shape[1] // QUERY_PER_KEY

    def wq_copy(i):
        at = pl.ds(pl.multiple_of(i * k_rows, k_rows), k_rows)
        return pltpu.make_async_copy(wq_hbm.at[at], wq.at[at], w_sem.at[i])

    wk_copy = pltpu.make_async_copy(wk_hbm, wkv.at[0], w_sem.at[QUERY_PER_KEY])
    wv_copy = pltpu.make_async_copy(wv_hbm, wkv.at[1], w_sem.at[QUERY_PER_KEY + 1])
    for i in range(QUERY_PER_KEY):
        wq_copy(i).start()
    wk_copy.start()
    wv_copy.start()

    barrier = pltpu.get_barrier_semaphore()
    for o in range(1, n):
        pl.semaphore_signal(
            barrier, inc=1, device_id=(lax.rem(me + o, n), mk), device_id_type=MESH
        )
    for o in range(1, nkv):
        pl.semaphore_signal(
            barrier, inc=1, device_id=(me, lax.rem(mk + o, nkv)), device_id_type=MESH
        )

    order = order_ref[...].astype(F32)
    groups = group_ref[...].astype(F32)
    plens = plen_ref[...].astype(F32)
    lane = iota((1, total), 1).astype(F32)

    own = iota((rows, 1), 0).astype(F32) + (me * rows).astype(F32)
    g_col = jnp.sum(jnp.where(order == own, groups, 0.0), axis=1, keepdims=True)
    all_g = iota((1, plens.shape[1]), 1).astype(F32)
    own_len = jnp.sum(jnp.where(all_g == g_col, plens, 0.0), axis=1, keepdims=True)
    own_tail = to_col(clen_ref[...].astype(F32))
    lengths[...] = jnp.broadcast_to(own_tail, lengths.shape)
    position = own_len + own_tail
    d_col = jnp.floor((g_col + 0.5) * (1.0 / lg))
    d_row = to_row(d_col)
    earlier = (d_col == d_row) & (iota((rows, rows), 0) < iota((rows, rows), 1))
    t_row = d_row * cap + jnp.sum(jnp.where(earlier, 1.0, 0.0), axis=0, keepdims=True)
    t_col = to_col(t_row)
    to_send = onehot(iota((n * cap, rows), 0).astype(F32) == t_row)
    from_return = onehot(iota((rows, n * cap), 1).astype(F32) == t_col)

    slot = iota((slots, 1), 0).astype(F32)
    slot_g = jnp.floor((slot + 0.5) * (1.0 / GROUP_CAPACITY))
    slot_k = slot - slot_g * GROUP_CAPACITY
    slot_g = slot_g + (me * lg).astype(F32)
    start = jnp.sum(jnp.where(groups < slot_g, 1.0, 0.0), axis=1, keepdims=True)
    count = jnp.sum(jnp.where(groups == slot_g, 1.0, 0.0), axis=1, keepdims=True)
    r_col = jnp.sum(jnp.where(lane == start + slot_k, order, 0.0), axis=1, keepdims=True)
    live = slot_k < count
    s_col = jnp.where(live, jnp.floor((r_col + 0.5) * (1.0 / rows)), -1.0)
    same = (s_col == to_row(s_col)) & (to_row(r_col) < r_col)
    u_col = jnp.where(
        live, s_col * cap + jnp.sum(jnp.where(same, 1.0, 0.0), axis=1, keepdims=True), -1.0
    )
    from_query = onehot(iota((slots, n * cap), 1).astype(F32) == u_col)
    to_return = onehot(iota((n * cap, slots), 0).astype(F32) == to_row(u_col))

    half = HEAD_SIZE // 2
    lane_h = iota((1, HEAD_SIZE), 1)
    upper = lane_h >= half
    freq_index = jnp.where(upper, lane_h - half, lane_h).astype(F32)
    freq = jnp.exp(-math.log(THETA) * 2.0 * freq_index / HEAD_SIZE)
    angle = position * freq
    cosine = jnp.cos(angle)
    sine = jnp.where(upper, jnp.sin(angle), -jnp.sin(angle))

    h_copy.wait()
    h32 = hidden[...].astype(F32)
    inv = lax.rsqrt(jnp.mean(h32 * h32, axis=1, keepdims=True) + EPS)
    normed[...] = (h32 * inv * gain_ref[...].astype(F32)[None, :]).astype(BF16)

    def turned(y, head):
        x = y[:, head * HEAD_SIZE : (head + 1) * HEAD_SIZE]
        return (x * cosine + pltpu.roll(x, half, 1) * sine).astype(BF16)

    def project(i, carry):
        wq_copy(i).wait()
        at = pl.ds(pl.multiple_of(i * k_rows, k_rows), k_rows)
        acc_q[...] += jnp.dot(normed[:, at], wq[at, :], preferred_element_type=F32)
        return carry

    acc_q[...] = jnp.zeros(acc_q.shape, F32)
    lax.fori_loop(0, 3, project, 0)
    for g in range(lg):
        pltpu.make_async_copy(pk_hbm.at[g], pk.at[g], pk_sem.at[g]).start()
        pltpu.make_async_copy(pv_hbm.at[g], pv.at[g], pv_sem.at[g]).start()
        if g == 0:
            pltpu.make_async_copy(ck_hbm, ck, ck_sem).start()
            pltpu.make_async_copy(cv_hbm, cv, cv_sem).start()
    lax.fori_loop(3, QUERY_PER_KEY, project, 0)
    for head in range(heads):
        query[:, head * HEAD_SIZE : (head + 1) * HEAD_SIZE] = turned(acc_q, head)

    sendq[...] = jnp.dot(to_send, query[...], preferred_element_type=F32).astype(BF16)
    pl.semaphore_wait(barrier, n - 1 + nkv - 1)

    def q_copy(o):
        to = lax.rem(me + o, n)
        return pltpu.make_async_remote_copy(
            src_ref=sendq.at[pl.ds(pl.multiple_of(to * cap, cap), cap)],
            dst_ref=recvq.at[pl.ds(pl.multiple_of(me * cap, cap), cap)],
            send_sem=q_send_sem.at[o],
            recv_sem=q_recv_sem.at[o],
            device_id=(to, mk),
            device_id_type=MESH,
        )

    def q_arrival(o):
        here = pl.ds(pl.multiple_of(lax.rem(me + n - o, n) * cap, cap), cap)
        return pltpu.make_async_remote_copy(
            src_ref=sendq.at[here],
            dst_ref=recvq.at[here],
            send_sem=q_send_sem.at[o],
            recv_sem=q_recv_sem.at[o],
            device_id=(lax.rem(me + o, n), mk),
            device_id_type=MESH,
        )

    def o_copy(k, o):
        to = lax.rem(me + o, n)
        return pltpu.make_async_remote_copy(
            src_ref=sendo.at[k, pl.ds(pl.multiple_of(to * cap, cap), cap)],
            dst_ref=recvo.at[k, pl.ds(pl.multiple_of(me * cap, cap), cap)],
            send_sem=o_send_sem.at[k, o],
            recv_sem=o_recv_sem.at[k, o],
            device_id=(to, mk),
            device_id_type=MESH,
        )

    def o_arrival(k, o):
        here = pl.ds(pl.multiple_of(lax.rem(me + n - o, n) * cap, cap), cap)
        return pltpu.make_async_remote_copy(
            src_ref=sendo.at[k, here],
            dst_ref=recvo.at[k, here],
            send_sem=o_send_sem.at[k, o],
            recv_sem=o_recv_sem.at[k, o],
            device_id=(lax.rem(me + o, n), mk),
            device_id_type=MESH,
        )

    mine = pl.ds(pl.multiple_of(me * cap, cap), cap)
    for o in range(1, n):
        q_copy(o).start()
    recvq[mine, :] = sendq[mine, :]

    wk_copy.wait()
    y = jnp.dot(normed[...], wkv[0], preferred_element_type=F32)
    for k in range(lkv):
        new_kv[0, :, k * HEAD_SIZE : (k + 1) * HEAD_SIZE] = turned(y, k)
    wv_copy.wait()
    new_kv[1] = jnp.dot(normed[...], wkv[1], preferred_element_type=F32).astype(BF16)
    pltpu.make_async_copy(ck_hbm, ck, ck_sem).wait()
    pltpu.make_async_copy(cv_hbm, cv, cv_sem).wait()
    block = CHUNK_ROWS
    width = block * tcap
    q_rows = QUERY_PER_KEY * block
    lanes = iota((block, HEAD_SIZE), 1)
    row_r = lax.rem(iota((q_rows, 1), 0), block)
    low = row_r * tcap
    col_t = iota((1, width), 1)

    def own_part(b, carry):
        at = pl.ds(pl.multiple_of(b * block, block), block)
        kv_at = pl.ds(pl.multiple_of(b * width, width), width)
        length = lengths[at, 0:1].astype(jnp.int32)
        length = jnp.concatenate([length] * QUERY_PER_KEY, axis=0)
        ok = (col_t >= low) & (col_t < low + length)
        for k in range(lkv):
            lse_tile = jnp.zeros((block, HEAD_SIZE), F32)
            ks = slice(k * HEAD_SIZE, (k + 1) * HEAD_SIZE)
            parts = []
            for h in range(QUERY_PER_KEY):
                head = k * QUERY_PER_KEY + h
                parts.append(query[at, head * HEAD_SIZE : (head + 1) * HEAD_SIZE])
            q = jnp.concatenate(parts, axis=0)
            new_k = new_kv[0, at, ks].astype(F32)
            new_v = new_kv[1, at, ks].astype(F32)
            s = lax.dot_general(
                q, ck[kv_at, ks], (((1,), (1,)), ((), ())), preferred_element_type=F32
            ) * scale
            s = jnp.where(ok, s, NEG)
            fresh = jnp.sum(
                q.astype(F32) * jnp.concatenate([new_k] * QUERY_PER_KEY, axis=0),
                axis=1,
                keepdims=True,
            ) * scale
            top = jnp.maximum(jnp.max(s, axis=1, keepdims=True), fresh)
            e = jnp.exp(s - top)
            fresh_e = jnp.exp(fresh - top)
            l = jnp.sum(e, axis=1, keepdims=True) + fresh_e
            acc = jnp.dot(e.astype(BF16), cv[kv_at, ks], preferred_element_type=F32)
            acc = acc + fresh_e.astype(BF16).astype(F32) * jnp.concatenate(
                [new_v] * QUERY_PER_KEY, axis=0
            )
            acc = acc / l
            lse = top + jnp.log(l)
            for h in range(QUERY_PER_KEY):
                head = k * QUERY_PER_KEY + h
                rs = slice(h * block, (h + 1) * block)
                tail_out[at, head * HEAD_SIZE : (head + 1) * HEAD_SIZE] = acc[rs]
                lse_tile = jnp.where(lanes == h, lse[rs], lse_tile)
            tail_lse[k, at, :] = lse_tile
        return carry

    lax.fori_loop(0, rows // block, own_part, 0)

    for o in range(1, n):
        q_arrival(o).wait_recv()
    for j in range(nkv):
        pltpu.make_async_copy(wo_hbm.at[:, pl.ds(j * oc, oc)], wo.at[j], wo_sem.at[j]).start()
    sel[...] = jnp.dot(from_query, recvq[...], preferred_element_type=F32).astype(BF16)

    cap_g = GROUP_CAPACITY
    lanes_g = iota((cap_g, HEAD_SIZE), 1)
    part_of = lanes_g // 32
    lane_of = lanes_g - part_of * 32
    col_p = iota((1, plen), 1).astype(F32)

    pc = QUERY_PER_KEY * HEAD_SIZE
    log2e = 1.0 / math.log(2.0)
    step = 2 if lg % 2 == 0 else 1

    def prompt_part(k, g):
        at = pl.ds(pl.multiple_of(g * cap_g, cap_g), cap_g)
        gid = (me * lg + g).astype(F32)
        length = jnp.sum(jnp.where(all_g == gid, plens, 0.0), axis=1, keepdims=True)
        ok = col_p < length
        ks = slice(k * HEAD_SIZE, (k + 1) * HEAD_SIZE)
        q = jnp.concatenate(
            [
                sel[at, k * pc + h * HEAD_SIZE : k * pc + (h + 1) * HEAD_SIZE]
                for h in range(QUERY_PER_KEY)
            ],
            axis=0,
        )
        s = lax.dot_general(
            q, pk[g, :, ks], (((1,), (1,)), ((), ())), preferred_element_type=F32
        ) * (scale * log2e)
        s = jnp.where(ok, s, NEG)
        top = jnp.max(s, axis=1, keepdims=True)
        e = jnp.exp2(s - top)
        l = jnp.sum(e, axis=1, keepdims=True)
        acc = jnp.dot(e.astype(BF16), pv[g, :, ks], preferred_element_type=F32) / l
        lse = top * math.log(2.0) + jnp.log(l)
        lse_tile = jnp.zeros((cap_g, HEAD_SIZE), F32)
        for h in range(QUERY_PER_KEY):
            rs = slice(h * cap_g, (h + 1) * cap_g)
            packed[at, h * HEAD_SIZE : (h + 1) * HEAD_SIZE] = acc[rs].astype(BF16)
            lse_tile = jnp.where(lane_of == h, lse[rs], lse_tile)
        hi = lse_tile.astype(BF16).astype(F32)
        mid = (lse_tile - hi).astype(BF16).astype(F32)
        low_part = lse_tile - hi - mid
        tile = jnp.where(part_of == 0, hi, jnp.where(part_of == 1, mid, low_part))
        packed[at, pc : pc + HEAD_SIZE] = jnp.where(part_of == 3, 0.0, tile).astype(BF16)

    for k in range(lkv):

        def prompt_step(j, carry, k=k):
            if k == 0:
                for a in range(step):
                    g = j * step + a
                    pltpu.make_async_copy(pk_hbm.at[g], pk.at[g], pk_sem.at[g]).wait()
                    pltpu.make_async_copy(pv_hbm.at[g], pv.at[g], pv_sem.at[g]).wait()
            for a in range(step):
                prompt_part(k, j * step + a)
            return carry

        lax.fori_loop(0, lg // step, prompt_step, 0)
        sendo[k] = jnp.dot(to_return, packed[...], preferred_element_type=F32).astype(BF16)
        for o in range(1, n):
            o_copy(k, o).start()
        recvo[k, mine, :] = sendo[k, mine, :]

    for j in range(nkv):
        pltpu.make_async_copy(
            wo_hbm.at[:, pl.ds(j * oc, oc)], wo.at[j], wo_sem.at[j]
        ).wait()

    for k in range(lkv):
        for o in range(1, n):
            o_arrival(k, o).wait_recv()
        got = jnp.dot(from_return, recvo[k], preferred_element_type=F32)
        parts = got[:, pc : pc + HEAD_SIZE]
        pre_lse = parts + pltpu.roll(parts, HEAD_SIZE - 32, 1) + pltpu.roll(parts, HEAD_SIZE - 64, 1)
        t_lse = tail_lse[k]
        top = jnp.maximum(pre_lse, t_lse)
        both = top + jnp.log(jnp.exp(pre_lse - top) + jnp.exp(t_lse - top))
        w_pre = jnp.exp(pre_lse - both)
        w_tail = jnp.exp(t_lse - both)
        for h in range(QUERY_PER_KEY):
            hs = slice(k * pc + h * HEAD_SIZE, k * pc + (h + 1) * HEAD_SIZE)
            attn[:, hs] = (
                w_pre[:, h : h + 1] * got[:, h * HEAD_SIZE : (h + 1) * HEAD_SIZE]
                + w_tail[:, h : h + 1] * tail_out[:, hs]
            ).astype(BF16)

    def z_copy(o):
        return pltpu.make_async_remote_copy(
            src_ref=zsend.at[o - 1],
            dst_ref=zrecv.at[o - 1],
            send_sem=z_send_sem.at[o - 1],
            recv_sem=z_recv_sem.at[o - 1],
            device_id=(me, lax.rem(mk + o, nkv)),
            device_id_type=MESH,
        )

    for o in range(1, nkv):
        zsend[o - 1] = jnp.dot(
            attn[...], wo[lax.rem(mk + o, nkv)], preferred_element_type=F32
        ).astype(BF16)
        z_copy(o).start()
    acc = jnp.dot(attn[...], wo[mk], preferred_element_type=F32)
    for o in range(1, nkv):
        z_copy(o).wait_recv()
        acc = acc + zrecv[o - 1].astype(F32)
    out_ref[...] = acc.astype(BF16)
    for o in range(1, n):
        q_copy(o).wait_send()
        for k in range(lkv):
            o_copy(k, o).wait_send()
    for o in range(1, nkv):
        z_copy(o).wait_send()


def attend(cap, n, nkv, cid, *arrays):
    (gain, order, group, plen, clen, hidden, wq, wk, wv, wo, pk, pv, ck, cv) = arrays
    rows, model = hidden.shape
    chunk = wk.shape[1]
    qc = wq.shape[1]
    oc = wo.shape[1] // nkv
    lg, positions = pk.shape[0], pk.shape[1]
    slots = lg * GROUP_CAPACITY
    lkv = chunk // HEAD_SIZE
    wide = QUERY_PER_KEY * HEAD_SIZE + HEAD_SIZE
    vmem = pl.BlockSpec(memory_space=pltpu.VMEM)
    hbm = pl.BlockSpec(memory_space=pl.ANY)
    dma = pltpu.SemaphoreType.DMA
    return pl.pallas_call(
        functools.partial(body, cap, n, nkv),
        out_shape=jax.ShapeDtypeStruct((rows, oc), BF16),
        in_specs=[vmem] * 5 + [hbm] * 9,
        out_specs=vmem,
        scratch_shapes=[
            pltpu.VMEM((rows, model), BF16),
            pltpu.VMEM((rows, model), BF16),
            pltpu.VMEM((model, qc), BF16),
            pltpu.VMEM((2, model, chunk), BF16),
            pltpu.VMEM((nkv, qc, oc), BF16),
            pltpu.VMEM(pk.shape, BF16),
            pltpu.VMEM(pv.shape, BF16),
            pltpu.VMEM(ck.shape, BF16),
            pltpu.VMEM(cv.shape, BF16),
            pltpu.VMEM((rows, qc), F32),
            pltpu.VMEM((rows, qc), BF16),
            pltpu.VMEM((2, rows, chunk), BF16),
            pltpu.VMEM((rows, HEAD_SIZE), F32),
            pltpu.VMEM((slots, qc), BF16),
            pltpu.VMEM((slots, wide), BF16),
            pltpu.VMEM((n * cap, qc), BF16),
            pltpu.VMEM((n * cap, qc), BF16),
            pltpu.VMEM((lkv, n * cap, wide), BF16),
            pltpu.VMEM((lkv, n * cap, wide), BF16),
            pltpu.VMEM((rows, qc), F32),
            pltpu.VMEM((lkv, rows, HEAD_SIZE), F32),
            pltpu.VMEM((rows, qc), BF16),
            pltpu.VMEM((nkv - 1, rows, oc), BF16),
            pltpu.VMEM((nkv - 1, rows, oc), BF16),
            dma,
            dma((QUERY_PER_KEY + 2,)),
            dma((nkv,)),
            dma((lg,)),
            dma((lg,)),
            dma,
            dma,
            dma((n,)),
            dma((n,)),
            dma((lkv, n)),
            dma((lkv, n)),
            dma((nkv - 1,)),
            dma((nkv - 1,)),
        ],
        compiler_params=pltpu.CompilerParams(
            collective_id=cid, has_side_effects=True, vmem_limit_bytes=62 * 1024 * 1024
        ),
        name="attend%d" % cap,
    )(*arrays)


def shards(
    hidden_in,
    norm_gain,
    w_query,
    key_projection,
    value_projection,
    w_out,
    pre_keys,
    prompt_values,
    continuation_keys,
    continuation_values,
    group_seq,
    request_order,
    pre_len,
    continuation_length,
):
    n = lax.axis_size("req")
    nkv = lax.axis_size("kv")
    rows = hidden_in.shape[0]
    lg = pre_keys.shape[0]
    width = continuation_keys.shape[2]
    arrays = (
        norm_gain,
        request_order[None, :],
        group_seq[None, :],
        pre_len[None, :],
        continuation_length[None, :],
        hidden_in,
        w_query,
        key_projection,
        value_projection,
        w_out,
        pre_keys,
        prompt_values,
        continuation_keys.reshape(-1, width),
        continuation_values.reshape(-1, width),
    )
    if rows <= FAST_CAPACITY:
        return attend(rows, n, nkv, 0, *arrays)
    pair = (request_order // rows) * n + group_seq // lg
    counts = jnp.sum(
        (pair[None, :] == jnp.arange(n * n, dtype=jnp.int32)[:, None]).astype(jnp.int32), axis=1
    )
    return lax.cond(
        jnp.max(counts) <= FAST_CAPACITY,
        functools.partial(attend, FAST_CAPACITY, n, nkv, 0),
        functools.partial(attend, rows, n, nkv, 1),
        *arrays,
    )


def solution(mesh):
    placed = (
        P("req", None),
        P(),
        P(None, "kv"),
        P(None, "kv"),
        P(None, "kv"),
        P("kv", None),
        P("req", None, "kv"),
        P("req", None, "kv"),
        P("req", None, "kv"),
        P("req", None, "kv"),
        P(),
        P(),
        P(),
        P("req"),
    )
    return jax.shard_map(
        shards, mesh=mesh, in_specs=placed, out_specs=P("req", "kv"), check_vma=False
    )
```

```python
import functools
import math

import jax
import jax.numpy as jnp
from jax import lax
from jax.experimental import pallas as pl
from jax.experimental.pallas import tpu as pltpu
from jax.sharding import PartitionSpec as P

HEAD_SIZE = 128
QUERY_PER_KEY = 5
GROUP_CAPACITY = 16
EPS = 1e-06
THETA = 1000000.0
NEG = -1e30
FAST_CAPACITY = 32
CHUNK_ROWS = 16

F32 = jnp.float32
BF16 = jnp.bfloat16
MESH = pl.DeviceIdType.MESH


def iota(shape, dim):
    return lax.broadcasted_iota(jnp.int32, shape, dim)


def to_row(col):
    n = col.shape[0]
    eye = iota((n, n), 0) == iota((n, n), 1)
    return jnp.sum(jnp.where(eye, col, 0.0), axis=0, keepdims=True)


def to_col(row):
    n = row.shape[1]
    eye = iota((n, n), 0) == iota((n, n), 1)
    return jnp.sum(jnp.where(eye, row, 0.0), axis=1, keepdims=True)


def onehot(mask):
    return jnp.where(mask, 1.0, 0.0).astype(BF16)


def body(
    cap,
    n,
    nkv,
    gain_ref,
    order_ref,
    group_ref,
    plen_ref,
    clen_ref,
    hidden_hbm,
    wq_hbm,
    wk_hbm,
    wv_hbm,
    wo_hbm,
    pk_hbm,
    pv_hbm,
    ck_hbm,
    cv_hbm,
    out_ref,
    hidden,
    normed,
    wq,
    wkv,
    wo,
    pk,
    pv,
    ck,
    cv,
    acc_q,
    query,
    new_kv,
    lengths,
    sel,
    packed,
    sendq,
    recvq,
    sendo,
    recvo,
    tail_out,
    tail_lse,
    attn,
    zsend,
    zrecv,
    h_sem,
    w_sem,
    wo_sem,
    pk_sem,
    pv_sem,
    ck_sem,
    cv_sem,
    q_send_sem,
    q_recv_sem,
    o_send_sem,
    o_recv_sem,
    z_send_sem,
    z_recv_sem,
):
    rows = hidden.shape[0]
    lg = pk.shape[0]
    plen = pk.shape[1]
    chunk = wkv.shape[2]
    lkv = chunk // HEAD_SIZE
    heads = lkv * QUERY_PER_KEY
    qc = heads * HEAD_SIZE
    tcap = ck.shape[0] // rows
    oc = out_ref.shape[1]
    slots = lg * GROUP_CAPACITY
    total = order_ref.shape[1]
    scale = 1.0 / math.sqrt(HEAD_SIZE)
    me = lax.axis_index("req")
    mk = lax.axis_index("kv")

    h_copy = pltpu.make_async_copy(hidden_hbm, hidden, h_sem)
    h_copy.start()
    k_rows = hidden.shape[1] // QUERY_PER_KEY

    def wq_copy(i):
        at = pl.ds(pl.multiple_of(i * k_rows, k_rows), k_rows)
        return pltpu.make_async_copy(wq_hbm.at[at], wq.at[at], w_sem.at[i])

    wk_copy = pltpu.make_async_copy(wk_hbm, wkv.at[0], w_sem.at[QUERY_PER_KEY])
    wv_copy = pltpu.make_async_copy(wv_hbm, wkv.at[1], w_sem.at[QUERY_PER_KEY + 1])
    for i in range(QUERY_PER_KEY):
        wq_copy(i).start()
    wk_copy.start()
    wv_copy.start()

    barrier = pltpu.get_barrier_semaphore()
    for o in range(1, n):
        pl.semaphore_signal(
            barrier, inc=1, device_id=(lax.rem(me + o, n), mk), device_id_type=MESH
        )
    for o in range(1, nkv):
        pl.semaphore_signal(
            barrier, inc=1, device_id=(me, lax.rem(mk + o, nkv)), device_id_type=MESH
        )

    order = order_ref[...].astype(F32)
    groups = group_ref[...].astype(F32)
    plens = plen_ref[...].astype(F32)
    lane = iota((1, total), 1).astype(F32)

    own = iota((rows, 1), 0).astype(F32) + (me * rows).astype(F32)
    g_col = jnp.sum(jnp.where(order == own, groups, 0.0), axis=1, keepdims=True)
    all_g = iota((1, plens.shape[1]), 1).astype(F32)
    own_len = jnp.sum(jnp.where(all_g == g_col, plens, 0.0), axis=1, keepdims=True)
    own_tail = to_col(clen_ref[...].astype(F32))
    lengths[...] = jnp.broadcast_to(own_tail, lengths.shape)
    position = own_len + own_tail
    d_col = jnp.floor((g_col + 0.5) * (1.0 / lg))
    d_row = to_row(d_col)
    earlier = (d_col == d_row) & (iota((rows, rows), 0) < iota((rows, rows), 1))
    t_row = d_row * cap + jnp.sum(jnp.where(earlier, 1.0, 0.0), axis=0, keepdims=True)
    t_col = to_col(t_row)
    to_send = onehot(iota((n * cap, rows), 0).astype(F32) == t_row)
    from_return = onehot(iota((rows, n * cap), 1).astype(F32) == t_col)

    slot = iota((slots, 1), 0).astype(F32)
    slot_g = jnp.floor((slot + 0.5) * (1.0 / GROUP_CAPACITY))
    slot_k = slot - slot_g * GROUP_CAPACITY
    slot_g = slot_g + (me * lg).astype(F32)
    start = jnp.sum(jnp.where(groups < slot_g, 1.0, 0.0), axis=1, keepdims=True)
    count = jnp.sum(jnp.where(groups == slot_g, 1.0, 0.0), axis=1, keepdims=True)
    r_col = jnp.sum(jnp.where(lane == start + slot_k, order, 0.0), axis=1, keepdims=True)
    live = slot_k < count
    s_col = jnp.where(live, jnp.floor((r_col + 0.5) * (1.0 / rows)), -1.0)
    same = (s_col == to_row(s_col)) & (to_row(r_col) < r_col)
    u_col = jnp.where(
        live, s_col * cap + jnp.sum(jnp.where(same, 1.0, 0.0), axis=1, keepdims=True), -1.0
    )
    from_query = onehot(iota((slots, n * cap), 1).astype(F32) == u_col)
    to_return = onehot(iota((n * cap, slots), 0).astype(F32) == to_row(u_col))

    half = HEAD_SIZE // 2
    lane_h = iota((1, HEAD_SIZE), 1)
    upper = lane_h >= half
    freq_index = jnp.where(upper, lane_h - half, lane_h).astype(F32)
    freq = jnp.exp(-math.log(THETA) * 2.0 * freq_index / HEAD_SIZE)
    angle = position * freq
    cosine = jnp.cos(angle)
    sine = jnp.where(upper, jnp.sin(angle), -jnp.sin(angle))

    h_copy.wait()
    h32 = hidden[...].astype(F32)
    inv = lax.rsqrt(jnp.mean(h32 * h32, axis=1, keepdims=True) + EPS)
    normed[...] = (h32 * inv * gain_ref[...].astype(F32)[None, :]).astype(BF16)

    def turned(y, head):
        x = y[:, head * HEAD_SIZE : (head + 1) * HEAD_SIZE]
        return (x * cosine + pltpu.roll(x, half, 1) * sine).astype(BF16)

    def project(i, carry):
        wq_copy(i).wait()
        at = pl.ds(pl.multiple_of(i * k_rows, k_rows), k_rows)
        acc_q[...] += jnp.dot(normed[:, at], wq[at, :], preferred_element_type=F32)
        return carry

    acc_q[...] = jnp.zeros(acc_q.shape, F32)
    lax.fori_loop(0, 3, project, 0)
    for g in range(lg):
        pltpu.make_async_copy(pk_hbm.at[g], pk.at[g], pk_sem.at[g]).start()
        pltpu.make_async_copy(pv_hbm.at[g], pv.at[g], pv_sem.at[g]).start()
        if g == 0:
            pltpu.make_async_copy(ck_hbm, ck, ck_sem).start()
            pltpu.make_async_copy(cv_hbm, cv, cv_sem).start()
    lax.fori_loop(3, QUERY_PER_KEY, project, 0)
    for head in range(heads):
        query[:, head * HEAD_SIZE : (head + 1) * HEAD_SIZE] = turned(acc_q, head)

    sendq[...] = jnp.dot(to_send, query[...], preferred_element_type=F32).astype(BF16)
    pl.semaphore_wait(barrier, n - 1 + nkv - 1)

    def q_copy(o):
        to = lax.rem(me + o, n)
        return pltpu.make_async_remote_copy(
            src_ref=sendq.at[pl.ds(pl.multiple_of(to * cap, cap), cap)],
            dst_ref=recvq.at[pl.ds(pl.multiple_of(me * cap, cap), cap)],
            send_sem=q_send_sem.at[o],
            recv_sem=q_recv_sem.at[o],
            device_id=(to, mk),
            device_id_type=MESH,
        )

    def q_arrival(o):
        here = pl.ds(pl.multiple_of(lax.rem(me + n - o, n) * cap, cap), cap)
        return pltpu.make_async_remote_copy(
            src_ref=sendq.at[here],
            dst_ref=recvq.at[here],
            send_sem=q_send_sem.at[o],
            recv_sem=q_recv_sem.at[o],
            device_id=(lax.rem(me + o, n), mk),
            device_id_type=MESH,
        )

    def o_copy(k, o):
        to = lax.rem(me + o, n)
        return pltpu.make_async_remote_copy(
            src_ref=sendo.at[k, pl.ds(pl.multiple_of(to * cap, cap), cap)],
            dst_ref=recvo.at[k, pl.ds(pl.multiple_of(me * cap, cap), cap)],
            send_sem=o_send_sem.at[k, o],
            recv_sem=o_recv_sem.at[k, o],
            device_id=(to, mk),
            device_id_type=MESH,
        )

    def o_arrival(k, o):
        here = pl.ds(pl.multiple_of(lax.rem(me + n - o, n) * cap, cap), cap)
        return pltpu.make_async_remote_copy(
            src_ref=sendo.at[k, here],
            dst_ref=recvo.at[k, here],
            send_sem=o_send_sem.at[k, o],
            recv_sem=o_recv_sem.at[k, o],
            device_id=(lax.rem(me + o, n), mk),
            device_id_type=MESH,
        )

    mine = pl.ds(pl.multiple_of(me * cap, cap), cap)
    for o in range(1, n):
        q_copy(o).start()
    recvq[mine, :] = sendq[mine, :]

    wk_copy.wait()
    y = jnp.dot(normed[...], wkv[0], preferred_element_type=F32)
    for k in range(lkv):
        new_kv[0, :, k * HEAD_SIZE : (k + 1) * HEAD_SIZE] = turned(y, k)
    wv_copy.wait()
    new_kv[1] = jnp.dot(normed[...], wkv[1], preferred_element_type=F32).astype(BF16)
    pltpu.make_async_copy(ck_hbm, ck, ck_sem).wait()
    pltpu.make_async_copy(cv_hbm, cv, cv_sem).wait()
    block = CHUNK_ROWS
    width = block * tcap
    q_rows = QUERY_PER_KEY * block
    lanes = iota((block, HEAD_SIZE), 1)
    row_r = lax.rem(iota((q_rows, 1), 0), block)
    low = row_r * tcap
    col_t = iota((1, width), 1)

    def own_part(b, carry):
        at = pl.ds(pl.multiple_of(b * block, block), block)
        kv_at = pl.ds(pl.multiple_of(b * width, width), width)
        length = lengths[at, 0:1].astype(jnp.int32)
        length = jnp.concatenate([length] * QUERY_PER_KEY, axis=0)
        ok = (col_t >= low) & (col_t < low + length)
        for k in range(lkv):
            lse_tile = jnp.zeros((block, HEAD_SIZE), F32)
            ks = slice(k * HEAD_SIZE, (k + 1) * HEAD_SIZE)
            parts = []
            for h in range(QUERY_PER_KEY):
                head = k * QUERY_PER_KEY + h
                parts.append(query[at, head * HEAD_SIZE : (head + 1) * HEAD_SIZE])
            q = jnp.concatenate(parts, axis=0)
            new_k = new_kv[0, at, ks].astype(F32)
            new_v = new_kv[1, at, ks].astype(F32)
            s = lax.dot_general(
                q, ck[kv_at, ks], (((1,), (1,)), ((), ())), preferred_element_type=F32
            ) * scale
            s = jnp.where(ok, s, NEG)
            fresh = jnp.sum(
                q.astype(F32) * jnp.concatenate([new_k] * QUERY_PER_KEY, axis=0),
                axis=1,
                keepdims=True,
            ) * scale
            top = jnp.maximum(jnp.max(s, axis=1, keepdims=True), fresh)
            e = jnp.exp(s - top)
            fresh_e = jnp.exp(fresh - top)
            l = jnp.sum(e, axis=1, keepdims=True) + fresh_e
            acc = jnp.dot(e.astype(BF16), cv[kv_at, ks], preferred_element_type=F32)
            acc = acc + fresh_e.astype(BF16).astype(F32) * jnp.concatenate(
                [new_v] * QUERY_PER_KEY, axis=0
            )
            acc = acc / l
            lse = top + jnp.log(l)
            for h in range(QUERY_PER_KEY):
                head = k * QUERY_PER_KEY + h
                rs = slice(h * block, (h + 1) * block)
                tail_out[at, head * HEAD_SIZE : (head + 1) * HEAD_SIZE] = acc[rs]
                lse_tile = jnp.where(lanes == h, lse[rs], lse_tile)
            tail_lse[k, at, :] = lse_tile
        return carry

    lax.fori_loop(0, rows // block, own_part, 0)

    for o in range(1, n):
        q_arrival(o).wait_recv()
    for j in range(nkv):
        pltpu.make_async_copy(wo_hbm.at[:, pl.ds(j * oc, oc)], wo.at[j], wo_sem.at[j]).start()
    sel[...] = jnp.dot(from_query, recvq[...], preferred_element_type=F32).astype(BF16)

    cap_g = GROUP_CAPACITY
    lanes_g = iota((cap_g, HEAD_SIZE), 1)
    part_of = lanes_g // 32
    lane_of = lanes_g - part_of * 32
    col_p = iota((1, plen), 1).astype(F32)

    pc = QUERY_PER_KEY * HEAD_SIZE
    log2e = 1.0 / math.log(2.0)
    step = 2 if lg % 2 == 0 else 1

    def prompt_part(k, g):
        at = pl.ds(pl.multiple_of(g * cap_g, cap_g), cap_g)
        gid = (me * lg + g).astype(F32)
        length = jnp.sum(jnp.where(all_g == gid, plens, 0.0), axis=1, keepdims=True)
        ok = col_p < length
        ks = slice(k * HEAD_SIZE, (k + 1) * HEAD_SIZE)
        q = jnp.concatenate(
            [
                sel[at, k * pc + h * HEAD_SIZE : k * pc + (h + 1) * HEAD_SIZE]
                for h in range(QUERY_PER_KEY)
            ],
            axis=0,
        )
        s = lax.dot_general(
            q, pk[g, :, ks], (((1,), (1,)), ((), ())), preferred_element_type=F32
        ) * (scale * log2e)
        s = jnp.where(ok, s, NEG)
        top = jnp.max(s, axis=1, keepdims=True)
        e = jnp.exp2(s - top)
        l = jnp.sum(e, axis=1, keepdims=True)
        acc = jnp.dot(e.astype(BF16), pv[g, :, ks], preferred_element_type=F32) / l
        lse = top * math.log(2.0) + jnp.log(l)
        lse_tile = jnp.zeros((cap_g, HEAD_SIZE), F32)
        for h in range(QUERY_PER_KEY):
            rs = slice(h * cap_g, (h + 1) * cap_g)
            packed[at, h * HEAD_SIZE : (h + 1) * HEAD_SIZE] = acc[rs].astype(BF16)
            lse_tile = jnp.where(lane_of == h, lse[rs], lse_tile)
        hi = lse_tile.astype(BF16).astype(F32)
        mid = (lse_tile - hi).astype(BF16).astype(F32)
        low_part = lse_tile - hi - mid
        tile = jnp.where(part_of == 0, hi, jnp.where(part_of == 1, mid, low_part))
        packed[at, pc : pc + HEAD_SIZE] = jnp.where(part_of == 3, 0.0, tile).astype(BF16)

    for k in range(lkv):

        def prompt_step(j, carry, k=k):
            if k == 0:
                for a in range(step):
                    g = j * step + a
                    pltpu.make_async_copy(pk_hbm.at[g], pk.at[g], pk_sem.at[g]).wait()
                    pltpu.make_async_copy(pv_hbm.at[g], pv.at[g], pv_sem.at[g]).wait()
            for a in range(step):
                prompt_part(k, j * step + a)
            return carry

        lax.fori_loop(0, lg // step, prompt_step, 0)
        sendo[k] = jnp.dot(to_return, packed[...], preferred_element_type=F32).astype(BF16)
        for o in range(1, n):
            o_copy(k, o).start()
        recvo[k, mine, :] = sendo[k, mine, :]

    for j in range(nkv):
        pltpu.make_async_copy(
            wo_hbm.at[:, pl.ds(j * oc, oc)], wo.at[j], wo_sem.at[j]
        ).wait()

    for k in range(lkv):
        for o in range(1, n):
            o_arrival(k, o).wait_recv()
        got = jnp.dot(from_return, recvo[k], preferred_element_type=F32)
        parts = got[:, pc : pc + HEAD_SIZE]
        pre_lse = parts + pltpu.roll(parts, HEAD_SIZE - 32, 1) + pltpu.roll(parts, HEAD_SIZE - 64, 1)
        t_lse = tail_lse[k]
        top = jnp.maximum(pre_lse, t_lse)
        both = top + jnp.log(jnp.exp(pre_lse - top) + jnp.exp(t_lse - top))
        w_pre = jnp.exp(pre_lse - both)
        w_tail = jnp.exp(t_lse - both)
        for h in range(QUERY_PER_KEY):
            hs = slice(k * pc + h * HEAD_SIZE, k * pc + (h + 1) * HEAD_SIZE)
            attn[:, hs] = (
                w_pre[:, h : h + 1] * got[:, h * HEAD_SIZE : (h + 1) * HEAD_SIZE]
                + w_tail[:, h : h + 1] * tail_out[:, hs]
            ).astype(BF16)

    def z_copy(source, slot, to):
        return pltpu.make_async_remote_copy(
            src_ref=zsend.at[source],
            dst_ref=zrecv.at[slot],
            send_sem=z_send_sem.at[source],
            recv_sem=z_recv_sem.at[slot],
            device_id=(me, to),
            device_id_type=MESH,
        )

    def partial(to):
        return jnp.dot(attn[...], wo[to], preferred_element_type=F32)

    if nkv == 4:
        side = mk // 2
        near_end = 3 * side
        far_end = 3 - near_end
        near = 1 + side
        far = 2 - side
        is_end = mk == near_end

        @pl.when(is_end)
        def _():
            zsend[0] = partial(far_end).astype(BF16)
            z_copy(0, 0, near).start()
            zsend[1] = partial(far).astype(BF16)
            z_copy(1, 1, far).start()
            zsend[2] = partial(near).astype(BF16)
            z_copy(2, 2, near).start()
            acc = partial(mk)
            z_copy(0, 2, near).wait_recv()
            acc = acc + zrecv[2].astype(F32)
            z_copy(1, 1, far).wait_recv()
            out_ref[...] = (acc + zrecv[1].astype(F32)).astype(BF16)
            z_copy(0, 0, near).wait_send()
            z_copy(1, 1, far).wait_send()
            z_copy(2, 2, near).wait_send()

        @pl.when(jnp.logical_not(is_end))
        def _():
            zsend[1] = partial(far).astype(BF16)
            z_copy(1, 3, far).start()
            zsend[2] = partial(near_end).astype(BF16)
            z_copy(2, 2, near_end).start()
            onward = partial(far_end)
            z_copy(0, 0, near_end).wait_recv()
            zsend[0] = (onward + zrecv[0].astype(F32)).astype(BF16)
            z_copy(0, 1, far_end).start()
            acc = partial(mk)
            z_copy(1, 3, far).wait_recv()
            acc = acc + zrecv[3].astype(F32)
            z_copy(2, 2, near_end).wait_recv()
            acc = acc + zrecv[2].astype(F32)
            z_copy(1, 1, far_end).wait_recv()
            out_ref[...] = (acc + zrecv[1].astype(F32)).astype(BF16)
            z_copy(0, 1, far_end).wait_send()
            z_copy(1, 3, far).wait_send()
            z_copy(2, 2, near_end).wait_send()

    else:
        for o in range(1, nkv):
            to = lax.rem(mk + o, nkv)
            zsend[o - 1] = partial(to).astype(BF16)
            z_copy(o - 1, o - 1, to).start()
        acc = partial(mk)
        for o in range(1, nkv):
            z_copy(o - 1, o - 1, lax.rem(mk + o, nkv)).wait_recv()
            acc = acc + zrecv[o - 1].astype(F32)
        out_ref[...] = acc.astype(BF16)
        for o in range(1, nkv):
            z_copy(o - 1, o - 1, lax.rem(mk + o, nkv)).wait_send()
    for o in range(1, n):
        q_copy(o).wait_send()
        for k in range(lkv):
            o_copy(k, o).wait_send()


def attend(cap, n, nkv, cid, *arrays):
    (gain, order, group, plen, clen, hidden, wq, wk, wv, wo, pk, pv, ck, cv) = arrays
    rows, model = hidden.shape
    chunk = wk.shape[1]
    qc = wq.shape[1]
    oc = wo.shape[1] // nkv
    lg, positions = pk.shape[0], pk.shape[1]
    slots = lg * GROUP_CAPACITY
    lkv = chunk // HEAD_SIZE
    wide = QUERY_PER_KEY * HEAD_SIZE + HEAD_SIZE
    vmem = pl.BlockSpec(memory_space=pltpu.VMEM)
    hbm = pl.BlockSpec(memory_space=pl.ANY)
    dma = pltpu.SemaphoreType.DMA
    return pl.pallas_call(
        functools.partial(body, cap, n, nkv),
        out_shape=jax.ShapeDtypeStruct((rows, oc), BF16),
        in_specs=[vmem] * 5 + [hbm] * 9,
        out_specs=vmem,
        scratch_shapes=[
            pltpu.VMEM((rows, model), BF16),
            pltpu.VMEM((rows, model), BF16),
            pltpu.VMEM((model, qc), BF16),
            pltpu.VMEM((2, model, chunk), BF16),
            pltpu.VMEM((nkv, qc, oc), BF16),
            pltpu.VMEM(pk.shape, BF16),
            pltpu.VMEM(pv.shape, BF16),
            pltpu.VMEM(ck.shape, BF16),
            pltpu.VMEM(cv.shape, BF16),
            pltpu.VMEM((rows, qc), F32),
            pltpu.VMEM((rows, qc), BF16),
            pltpu.VMEM((2, rows, chunk), BF16),
            pltpu.VMEM((rows, HEAD_SIZE), F32),
            pltpu.VMEM((slots, qc), BF16),
            pltpu.VMEM((slots, wide), BF16),
            pltpu.VMEM((n * cap, qc), BF16),
            pltpu.VMEM((n * cap, qc), BF16),
            pltpu.VMEM((lkv, n * cap, wide), BF16),
            pltpu.VMEM((lkv, n * cap, wide), BF16),
            pltpu.VMEM((rows, qc), F32),
            pltpu.VMEM((lkv, rows, HEAD_SIZE), F32),
            pltpu.VMEM((rows, qc), BF16),
            pltpu.VMEM((nkv - 1, rows, oc), BF16),
            pltpu.VMEM((nkv, rows, oc), BF16),
            dma,
            dma((QUERY_PER_KEY + 2,)),
            dma((nkv,)),
            dma((lg,)),
            dma((lg,)),
            dma,
            dma,
            dma((n,)),
            dma((n,)),
            dma((lkv, n)),
            dma((lkv, n)),
            dma((nkv - 1,)),
            dma((nkv,)),
        ],
        compiler_params=pltpu.CompilerParams(
            collective_id=cid, has_side_effects=True, vmem_limit_bytes=62 * 1024 * 1024
        ),
        name="attend%d" % cap,
    )(*arrays)


def shards(
    hidden_in,
    norm_gain,
    w_query,
    key_projection,
    value_projection,
    w_out,
    pre_keys,
    prompt_values,
    continuation_keys,
    continuation_values,
    group_seq,
    request_order,
    pre_len,
    continuation_length,
):
    n = lax.axis_size("req")
    nkv = lax.axis_size("kv")
    rows = hidden_in.shape[0]
    lg = pre_keys.shape[0]
    width = continuation_keys.shape[2]
    arrays = (
        norm_gain,
        request_order[None, :],
        group_seq[None, :],
        pre_len[None, :],
        continuation_length[None, :],
        hidden_in,
        w_query,
        key_projection,
        value_projection,
        w_out,
        pre_keys,
        prompt_values,
        continuation_keys.reshape(-1, width),
        continuation_values.reshape(-1, width),
    )
    if rows <= FAST_CAPACITY:
        return attend(rows, n, nkv, 0, *arrays)
    pair = (request_order // rows) * n + group_seq // lg
    counts = jnp.sum(
        (pair[None, :] == jnp.arange(n * n, dtype=jnp.int32)[:, None]).astype(jnp.int32), axis=1
    )
    return lax.cond(
        jnp.max(counts) <= FAST_CAPACITY,
        functools.partial(attend, FAST_CAPACITY, n, nkv, 0),
        functools.partial(attend, rows, n, nkv, 1),
        *arrays,
    )


def solution(mesh):
    placed = (
        P("req", None),
        P(),
        P(None, "kv"),
        P(None, "kv"),
        P(None, "kv"),
        P("kv", None),
        P("req", None, "kv"),
        P("req", None, "kv"),
        P("req", None, "kv"),
        P("req", None, "kv"),
        P(),
        P(),
        P(),
        P("req"),
    )
    return jax.shard_map(
        shards, mesh=mesh, in_specs=placed, out_specs=P("req", "kv"), check_vma=False
    )
```
